256 devices in a mesh: grp: 8 (over x, core), seq: 32 (over z, y).
Axes of the slice: x: 4, y: 4, z: 8, core: 2. Of those that a mesh axis runs over, the one named last changes fastest.
Arguments:
- prompt_keys: bfloat16 [8, 8192, 256], P('grp', 'seq')
- prompt_values: bfloat16 [8, 8192, 256], P('grp', 'seq'), may hold values from -6 to 6
- resp_queries: bfloat16 [8, 4096, 1792], P(None, ('seq', 'grp'))
- resp_keys: bfloat16 [8, 4096, 256], P(None, ('seq', 'grp')), may hold values from -6 to 6
- resp_values: bfloat16 [8, 4096, 256], P(None, ('seq', 'grp')), may hold values from -6 to 6
- segment_ids: int32 [8, 4096], P('grp', 'seq'), may hold values from 0 to 15, never falling along the last dimension, each value on 1 to 512 neighbouring positions
- prompt_lengths: int32 [8], P('grp'), may hold values from 4096 to 8192, as said below
Outputs:
- attended: bfloat16 [8, 4096, 1792], P('grp', 'seq')
The draws below stay inside these ranges and needn't reach their ends.
Inputs may be any that keep to these rules, and one draw needn't show every extreme that they name: `prompt_lengths`: between half of 8192 and 8192; some group uses all 8192 slots.
All inputs are finite; a program needn't handle non-finite values.
Results may differ from the reference program's by a relative error of at most 0.0095.
Values may be sent and summed in bfloat16 or wider, within the bound.
A program may use at most 64 MiB of HBM per device.

```python
import math
import jax
import jax.numpy as jnp
import numpy as np
from jax import lax

HD = 128
H = 14
KVH = 2
LMAX = 512
RESP = 16
GROUPS = 8
P_SIZE = 8192
RT = 4096


def shared_keys(key):
    base = jnp.clip(jax.random.normal(key, (GROUPS, P_SIZE, KVH, HD), jnp.float32), -6.0, 6.0)
    strengths = 10.0 * (1.0 + jnp.arange(4, dtype=jnp.float32))
    factors = 1.0 - 2.0 / (strengths * math.sqrt(HD))
    leading = base[:, 0:8:2]
    following = leading * factors[None, :, None, None]
    paired = jnp.stack([leading, following], axis=2).reshape(GROUPS, 8, KVH, HD)
    return base.at[:, :8].set(paired)


def draw_prompt_keys(key, part):
    keys_all = shared_keys(key)
    return keys_all.reshape(GROUPS, P_SIZE, KVH * HD).astype(jnp.bfloat16)


def draw_resp_queries(key, part):
    key = jax.random.fold_in(key, 5)
    heads_group = H // KVH
    drawn = jnp.clip(jax.random.normal(key, (GROUPS, RT, KVH, heads_group, HD), jnp.float32), -6.0, 6.0)
    return drawn.reshape(GROUPS, RT, H * HD).astype(jnp.bfloat16)


def draw_prompt_lengths(key, part):
    key = jax.random.fold_in(key, 7)
    first_key, second_key = jax.random.split(key)
    drawn = jax.random.randint(first_key, (GROUPS,), P_SIZE // 2, P_SIZE + 1, dtype=jnp.int32)
    chosen = jax.random.randint(second_key, (), 0, GROUPS, dtype=jnp.int32)
    return jnp.where(jnp.arange(GROUPS, dtype=jnp.int32) == chosen, P_SIZE, drawn).astype(jnp.int32)


def block_levels(own_key, extent, pieces, low, high):
    loudness, own = 1.0, jax.random.fold_in(own_key, 6)
    for axis_at, shards_of in pieces:
        heights = jnp.exp(jax.random.uniform(jax.random.fold_in(own, axis_at), (shards_of,), jnp.float32, low / len(pieces), high / len(pieces)))
        loudness = loudness * jnp.repeat(heights, extent[axis_at] // shards_of).reshape([-1 if axis == axis_at else 1 for axis in range(len(extent))])
    return loudness


def split_up(count, total, most, lean):
    weights = [(1 << 20) // math.isqrt(standing ** lean) + 1 for standing in range(2, count + 1)]
    surplus, given = total - most - (count - 1), [1] * (count - 1)
    while surplus > 0:
        free = [i for i in range(count - 1) if given[i] < most]
        whole, budget = sum([weights[i] for i in free]), surplus
        for i in free:
            addition = min(most - given[i], max(1, budget * weights[i] // whole), surplus)
            given[i] = given[i] + addition
            surplus = surplus - addition
    return np.array([most] + given)


def uneven(own_key, amount, total, limit, skew):
    if amount == 2:
        one = jax.random.randint(own_key, (), max(1, total - limit), min(limit, total - 1) + 1)
        return jnp.stack([one, total - one])
    lengths = jnp.asarray(split_up(amount, total, limit, skew), jnp.int32)
    couples = (amount - 1) // 2
    donor, taker = lengths[1:1 + 2 * couples:2], lengths[2:2 + 2 * couples:2]
    room = jnp.minimum(donor - 1, limit - taker)
    passed = jax.random.randint(jax.random.fold_in(own_key, 1), (couples,), 0, 1 << 20) % (room + 1)
    lengths = lengths.at[1:1 + 2 * couples:2].set(donor - passed).at[2:2 + 2 * couples:2].set(taker + passed)
    return lengths[jax.random.permutation(jax.random.fold_in(own_key, 2), amount)]


def bell_draw(key, extent, spread, bound, cuts=(), held_as=jnp.bfloat16):
    values = jax.random.normal(key, extent, jnp.float32) * spread
    if len(cuts) > 0:
        values = block_levels(key, extent, cuts, -0.22, 0.18) * values
    return jnp.clip(values, min=-bound, max=bound).astype(held_as)


def setup_inputs(seed: int = 0) -> dict:
    splits = jax.random.split(jax.random.key(seed), 8)
    return {
        "prompt_keys": draw_prompt_keys(jax.random.fold_in(splits[7], 71), 0),
        "prompt_values": bell_draw(splits[1], (GROUPS, P_SIZE, KVH * HD), 1.0, 6.0, ((0, 8), (1, 32))),
        "resp_queries": draw_resp_queries(jax.random.fold_in(splits[7], 71), 0),
        "resp_keys": bell_draw(splits[3], (GROUPS, RT, KVH * HD), 1.0, 6.0, ((1, 256),)),
        "resp_values": bell_draw(splits[4], (GROUPS, RT, KVH * HD), 1.0, 6.0, ((1, 256),)),
        "segment_ids": jax.vmap(lambda own: jnp.searchsorted(jnp.cumsum(uneven(own, RESP, RT, LMAX, 2)), jnp.arange(RT), side="right"))(jax.random.split(splits[5], GROUPS)).reshape((GROUPS, RT)).astype(jnp.int32),
        "prompt_lengths": draw_prompt_lengths(jax.random.fold_in(splits[7], 71), 0),
    }


masked_score = -1e+30

def group_attention(queries, prompt_k, prompt_v, reply_k, reply_v, segments, prompt_limit):
    total_rows = queries.shape[0]
    block = math.gcd(total_rows, 128)
    heads_group = H // KVH
    scale = 1.0 / math.sqrt(HD)
    key_all = jnp.concatenate([prompt_k, reply_k], axis=0).astype(jnp.float32).reshape(P_SIZE + total_rows, KVH, HD)
    value_all = jnp.concatenate([prompt_v, reply_v], axis=0).astype(jnp.float32).reshape(P_SIZE + total_rows, KVH, HD)
    starts = jnp.searchsorted(segments, segments, side='left').astype(jnp.int32)
    key_pos = jnp.arange(P_SIZE + total_rows, dtype=jnp.int32)
    reply_pos = key_pos - P_SIZE
    in_prompt = key_pos < P_SIZE
    blocked = queries.astype(jnp.float32).reshape(total_rows // block, block, KVH, heads_group, HD)

    def one_block(items):
        query_block, index = items
        row_pos = index * block + jnp.arange(block, dtype=jnp.int32)
        row_start = lax.dynamic_slice(starts, (index * block,), (block,))
        reply_ok = (reply_pos[None, :] >= row_start[:, None]) & (reply_pos[None, :] <= row_pos[:, None])
        valid = jnp.where(in_prompt[None, :], (key_pos < prompt_limit)[None, :], reply_ok)
        scores = jnp.einsum('rkgd,nkd->kgrn', query_block, key_all) * scale
        scores = jnp.where(valid, scores, masked_score)
        maxima = lax.optimization_barrier(jnp.max(scores, axis=-1))
        weights = jnp.where(valid, jnp.exp(scores - maxima[..., None]), 0.0)
        totals = lax.optimization_barrier(jnp.sum(weights, axis=-1))
        rounded = lax.optimization_barrier(weights.astype(jnp.bfloat16))
        summed = jnp.einsum('kgrn,nkd->rkgd', rounded.astype(jnp.float32), value_all, precision=lax.Precision.HIGHEST)
        output = summed / jnp.transpose(totals, (2, 0, 1))[..., None]
        return output.reshape(block, H * HD).astype(jnp.bfloat16)
    result = lax.map(one_block, (blocked, jnp.arange(total_rows // block, dtype=jnp.int32)))
    return result.reshape(total_rows, H * HD)

def reference(prompt_keys, prompt_values, resp_queries, resp_keys, resp_values, segment_ids, prompt_lengths):

    def per_group(items):
        return group_attention(*items)
    return lax.map(per_group, (resp_queries, prompt_keys, prompt_values, resp_keys, resp_values, segment_ids, prompt_lengths))
```

```python
import math

import jax
import jax.numpy as jnp
from jax import lax
from jax.experimental import pallas as pl
from jax.experimental.pallas import tpu as pltpu
from jax.sharding import PartitionSpec as P

HD = 128
H = 14
KVH = 2
HG = H // KVH
WIDE = HG * HD
XS, YS, ZS = 4, 4, 8
ROWS = 256
WIN = 3 * ROWS
SHARD = 256
HALF = 2 * SHARD
CHUNK = 2 * HALF
KEYS = WIN + ZS * CHUNK
MASKED = -1e30
LOG2 = math.log2(math.e) / math.sqrt(HD)
DELTA = (0, -1, 1, -2, 2, -3, 3, 4)
AHEAD = {0: 1, 1: 3, 3: 5, 5: 7}
BEHIND = {0: 2, 2: 4, 4: 6, 6: 7}
STEPS = ((0, 1), (1, 3), (3, 5), (5, 8))
MESH = pl.DeviceIdType.MESH


def kernel(
    pk, pv, rq, rk, rv, seg, plen, out,
    qbuf, kbuf, vbuf, segsrc, segbuf, acc, peak, obuf, bias0,
    q_send, q_recv, rkv_recv, st_send, st_recv,
    ring_send, ring_recv, sib_send, sib_recv,
    fw_send, fw_recv, o_send, o_recv,
):
    gi = lax.axis_index("grp")
    si = lax.axis_index("seq")
    x, c = lax.div(gi, 2), lax.rem(gi, 2)
    z, y = lax.div(si, YS), lax.rem(si, YS)
    yh, yl = lax.div(y, 2), lax.rem(y, 2)
    zn, zp = lax.rem(z + 1, ZS), lax.rem(z + ZS - 1, ZS)
    mine = yh == c
    ahead = (gi, zn * YS + y)
    behind = (gi, zp * YS + y)
    sibling = (2 * x + 1 - c, si)
    next_one = (2 * x + 1 - c, jnp.where(c == 0, si, zn * YS + y))
    prev_one = (2 * x + 1 - c, jnp.where(c == 1, si, zp * YS + y))

    barrier = pltpu.get_barrier_semaphore()

    def greet(i, carry):
        s, g = lax.div(i, 8), lax.rem(i, 8)
        who = z * YS + 2 * c + s

        @pl.when(jnp.logical_or(g != gi, who != si))
        def _():
            pl.semaphore_signal(barrier, inc=1, device_id=(g, who), device_id_type=MESH)

        return carry

    lax.fori_loop(0, 16, greet, 0)
    for who in (ahead, behind, sibling, prev_one):
        pl.semaphore_signal(barrier, inc=1, device_id=who, device_id_type=MESH)
    segsrc[...] = jnp.full((8, 128), plen[0], jnp.int32)
    segsrc[0:1, :] = seg[...]
    pl.semaphore_wait(barrier, jnp.where(mine, 19, 20))

    def remote(src, dst, send, recv, who):
        return pltpu.make_async_remote_copy(
            src_ref=src, dst_ref=dst, send_sem=send, recv_sem=recv,
            device_id=who, device_id_type=MESH,
        )

    def put(src, dst, send, recv, who, here):
        @pl.when(here)
        def _():
            pltpu.make_async_copy(src, dst, recv).start()

        @pl.when(jnp.logical_not(here))
        def _():
            remote(src, dst, send, recv, who).start()

    def sent(src, dst, send, recv, who, here):
        @pl.when(jnp.logical_not(here))
        def _():
            remote(src, dst, send, recv, who).wait_send()

    def arrived(ref, sem):
        pltpu.make_async_copy(ref, ref, sem).wait()

    def keys_at(start, count):
        return kbuf.at[pl.ds(start, count), :]

    def values_at(start, count):
        return vbuf.at[pl.ds(start, count), pl.ds(0, HD)]

    own_at = pl.multiple_of(WIN + y * SHARD, SHARD)

    def staged(h):
        who = (2 * x + yh, z * YS + 2 * c + h)
        here = jnp.logical_and(mine, yl == h)
        cols = pl.ds(h * HD, HD)
        return (
            (pk.at[0, :, cols], keys_at(own_at, SHARD), st_send.at[0, h], st_recv.at[0], who, here),
            (pv.at[0, :, cols], values_at(own_at, SHARD), st_send.at[1, h], st_recv.at[1], who, here),
            (segsrc, segbuf.at[2, yl], st_send.at[2, h], st_recv.at[2], who, here),
        )

    for part in range(3):
        for h in range(2):
            put(*staged(h)[part])

    row_at = pl.multiple_of(yl * 128 + gi * 16, 16)

    def queried(i):
        tx = lax.rem(x + 1 + lax.div(i, 4), XS)
        ty = lax.rem(y + 1 + lax.rem(i, 4), YS)
        th = lax.div(ty, 2)
        tl = lax.rem(ty, 2)
        g = 2 * tx + th
        who = (2 * tx + yh, z * YS + ty)
        here = jnp.logical_and(mine, i == 15)
        wide = pl.ds(pl.multiple_of(tl * WIDE, 128), WIDE)
        cols = pl.ds(pl.multiple_of(tl * HD, 128), HD)
        at = pl.multiple_of(2 * ROWS + row_at, 16)
        return (
            (rq.at[g, :, wide], qbuf.at[pl.ds(row_at, 16), :], q_send.at[0, i], q_recv, who, here),
            (rk.at[g, :, cols], keys_at(at, 16), q_send.at[1, i], rkv_recv.at[0], who, here),
            (rv.at[g, :, cols], values_at(at, 16), q_send.at[2, i], rkv_recv.at[1], who, here),
        )

    def send_queries(i, carry):
        for item in queried(i):
            put(*item)
        return carry

    lax.fori_loop(0, 16, send_queries, 0)

    half_c = pl.multiple_of(c * HALF, HALF)
    other_c = pl.multiple_of((1 - c) * HALF, HALF)

    def chunk_at(kind, r, off):
        start = pl.multiple_of(WIN + r * CHUNK + off, SHARD)
        return keys_at(start, HALF) if kind == 0 else values_at(start, HALF)

    def onward(kind, r):
        moves = []
        if r in AHEAD and not (kind == 1 and AHEAD[r] == 7):
            moves.append((AHEAD[r], ahead))
        if r in BEHIND and not (kind == 0 and BEHIND[r] == 7):
            moves.append((BEHIND[r], behind))
        copies = [
            remote(chunk_at(kind, r, half_c), chunk_at(kind, d, half_c),
                   ring_send.at[kind, d], ring_recv.at[kind, d], who)
            for d, who in moves
        ]
        copies.append(
            remote(chunk_at(kind, r, half_c), chunk_at(kind, r, half_c),
                   sib_send.at[kind, r], sib_recv.at[kind, r], sibling)
        )
        return copies

    def relay(r):
        for kind in range(2):
            sem = st_recv.at[kind] if r == 0 else ring_recv.at[kind, r]
            arrived(chunk_at(kind, r, half_c), sem)
            for copy in onward(kind, r):
                copy.start()

    def from_sibling(r):
        for kind in range(2):
            arrived(chunk_at(kind, r, other_c), sib_recv.at[kind, r])

    relay(0)

    def block_refs(slot):
        return (keys_at(slot * ROWS, ROWS), values_at(slot * ROWS, ROWS), segbuf.at[slot])

    def forwards():
        mine_refs = block_refs(2)
        return [
            remote(mine_refs[k], block_refs(slot)[k], fw_send.at[slot, k], fw_recv.at[slot, k], who)
            for slot, who in ((1, next_one), (0, ahead))
            for k in range(3)
        ]

    arrived(segbuf.at[2], st_recv.at[2])
    arrived(block_refs(2)[0], rkv_recv.at[0])
    arrived(block_refs(2)[1], rkv_recv.at[1])
    for copy in forwards():
        copy.start()

    def ones(i, carry):
        vbuf[pl.ds(pl.multiple_of(i * 256, 256), 256), HD:] = jnp.ones((256, HD), jnp.bfloat16)
        return carry

    lax.fori_loop(0, KEYS // 256, ones, 0)

    limit = segbuf[2, 0, 1:2, :]
    lane = lax.broadcasted_iota(jnp.int32, (1, 128), 1)

    def prompt_bias(r):
        base = lax.rem(z + ZS + DELTA[r], ZS) * CHUNK
        return [
            jnp.where(base + j * 128 + lane < limit, 0.0, MASKED).astype(jnp.float32)
            for j in range(CHUNK // 128)
        ]

    for slot in range(2):
        for k in range(3):
            arrived(block_refs(slot)[k], fw_recv.at[slot, k])

    first = 512 * z + 256 * c - 512
    row = lax.broadcasted_iota(jnp.int32, (128, 128), 0)
    col = lax.broadcasted_iota(jnp.int32, (128, 128), 1)
    for a in range(2):
        ids = jnp.broadcast_to(segbuf[2, a, 0:1, :].astype(jnp.float32), (128, 128))
        ids = jnp.transpose(ids)
        for j in range(WIN // 128):
            theirs = segbuf[j // 2, j % 2, 0:1, :].astype(jnp.float32)
            before = (j * 128 + col <= 512 + a * 128 + row) & (first + j * 128 + col >= 0)
            bias0[a * 128:(a + 1) * 128, j * 128:(j + 1) * 128] = jnp.where(
                before & (ids == theirs), 0.0, MASKED
            ).astype(jnp.float32)

    from_sibling(0)
    arrived(qbuf, q_recv)

    def weigh(lo, count, rows, h, bias):
        q = qbuf[rows, h * HD:(h + 1) * HD]
        s = lax.dot_general(
            q, kbuf[lo:lo + count, :], (((1,), (1,)), ((), ())),
            preferred_element_type=jnp.float32,
        )
        return s + bias

    def numerators(s, top):
        return jnp.exp2((s - top[:, :1]) * LOG2).astype(jnp.bfloat16)

    def product(p, lo, count):
        return jnp.dot(p, vbuf[lo:lo + count, :], preferred_element_type=jnp.float32)

    for step, (a, b) in enumerate(STEPS):
        last = step == len(STEPS) - 1
        pieces = [piece for r in range(a, b) for piece in prompt_bias(r)]
        bias = jnp.concatenate(pieces, axis=1)
        if step == 0:
            lo, count = 0, WIN + CHUNK
            bias = jnp.concatenate(
                [bias0[...], jnp.broadcast_to(bias, (ROWS, CHUNK))], axis=1
            )
        else:
            lo, count = WIN + a * CHUNK, (b - a) * CHUNK
            for r in range(a, b):
                from_sibling(r)
        if not last:
            for h in range(HG):
                if h == 3:
                    relay(b)
                    relay(b + 1)
                if h == 6 and step == 2:
                    relay(7)
                rows = slice(0, ROWS)
                s = weigh(lo, count, rows, h, bias)
                top = jnp.max(s, axis=1, keepdims=True)
                if step == 0:
                    top = jnp.broadcast_to(top, (ROWS, HD))
                    acc[h] = product(numerators(s, top), lo, count)
                else:
                    old = peak[h]
                    top = jnp.maximum(old, top)
                    fade = jnp.exp2((old - top) * LOG2)
                    got = product(numerators(s, top), lo, count)
                    acc[h, :, :HD] = acc[h, :, :HD] * fade + got[:, :HD]
                    acc[h, :, HD:] = acc[h, :, HD:] * fade + got[:, HD:]
                peak[h] = top
        else:
            for a_half in range(2):
                for h in range(HG):
                    rows = slice(a_half * 128, a_half * 128 + 128)
                    s = weigh(lo, count, rows, h, bias)
                    old = peak[h, rows, :]
                    top = jnp.maximum(old, jnp.max(s, axis=1, keepdims=True))
                    fade = jnp.exp2((old - top) * LOG2)
                    got = product(numerators(s, top), lo, count)
                    weighted = acc[h, rows, :HD] * fade + got[:, :HD]
                    total = acc[h, rows, HD:] * fade + got[:, HD:]
                    obuf[a_half, h] = (weighted / total).astype(jnp.bfloat16)
                    put(*answer(obuf, out, o_send, o_recv, a_half, h, x, c, z, yh, yl, mine))

    for a_half in range(2):
        for h in range(HG):
            sent(*answer(obuf, out, o_send, o_recv, a_half, h, x, c, z, yh, yl, mine))
    for h in range(2):
        for item in staged(h):
            sent(*item)

    def settle(i, carry):
        for item in queried(i):
            sent(*item)
        return carry

    lax.fori_loop(0, 16, settle, 0)
    for r in range(ZS):
        for kind in range(2):
            for copy in onward(kind, r):
                copy.wait_send()
    for copy in forwards():
        copy.wait_send()
    arrived(out, o_recv)


def answer(obuf, out, o_send, o_recv, a_half, h, x, c, z, yh, yl, mine):
    who = (2 * x + yh, z * YS + 2 * c + a_half)
    here = jnp.logical_and(mine, yl == a_half)
    cols = pl.ds(pl.multiple_of(yl * WIDE + h * HD, 128), HD)
    return (obuf.at[a_half, h], out.at[0, :, cols], o_send.at[a_half, h], o_recv, who, here)


def body(
    prompt_keys, prompt_values, resp_queries, resp_keys, resp_values, segment_ids, prompt_lengths
):
    dma = pltpu.SemaphoreType.DMA
    held = pl.BlockSpec(memory_space=pl.ANY)
    return pl.pallas_call(
        kernel,
        out_shape=jax.ShapeDtypeStruct((1, 128, H * HD), jnp.bfloat16),
        in_specs=[held] * 5
        + [pl.BlockSpec(memory_space=pltpu.VMEM), pl.BlockSpec(memory_space=pltpu.SMEM)],
        out_specs=held,
        scratch_shapes=[
            pltpu.VMEM((ROWS, WIDE), jnp.bfloat16),
            pltpu.VMEM((KEYS, HD), jnp.bfloat16),
            pltpu.VMEM((KEYS, 2 * HD), jnp.bfloat16),
            pltpu.VMEM((8, 128), jnp.int32),
            pltpu.VMEM((3, 2, 8, 128), jnp.int32),
            pltpu.VMEM((HG, ROWS, 2 * HD), jnp.float32),
            pltpu.VMEM((HG, ROWS, HD), jnp.float32),
            pltpu.VMEM((2, HG, 128, HD), jnp.bfloat16),
            pltpu.VMEM((ROWS, WIN), jnp.float32),
            dma((3, 16)),
            dma,
            dma((2,)),
            dma((3, 2)),
            dma((3,)),
            dma((2, ZS)),
            dma((2, ZS)),
            dma((2, ZS)),
            dma((2, ZS)),
            dma((2, 3)),
            dma((2, 3)),
            dma((2, HG)),
            dma,
        ],
        compiler_params=pltpu.CompilerParams(
            collective_id=0, has_side_effects=True, vmem_limit_bytes=50 << 20
        ),
        name="shared_prompt_attention",
    )(prompt_keys, prompt_values, resp_queries, resp_keys, resp_values, segment_ids, prompt_lengths)


def solution(mesh):
    in_specs = (
        P("grp", "seq", None),
        P("grp", "seq", None),
        P(None, ("seq", "grp"), None),
        P(None, ("seq", "grp"), None),
        P(None, ("seq", "grp"), None),
        P("grp", "seq"),
        P("grp"),
    )
    out_specs = P("grp", "seq", None)
    return jax.shard_map(body, mesh=mesh, in_specs=in_specs, out_specs=out_specs, check_vma=False)
```

```python
import math

import jax
import jax.numpy as jnp
from jax import lax
from jax.experimental import pallas as pl
from jax.experimental.pallas import tpu as pltpu
from jax.sharding import PartitionSpec as P

HD = 128
H = 14
KVH = 2
HG = H // KVH
WIDE = HG * HD
XS, YS, ZS = 4, 4, 8
ROWS = 256
WIN = 3 * ROWS
SHARD = 256
HALF = 2 * SHARD
CHUNK = 2 * HALF
KEYS = WIN + ZS * CHUNK
MASKED = -1e30
LOG2 = math.log2(math.e) / math.sqrt(HD)
DELTA = (0, -1, 1, -2, 2, -3, 3, 4)
AHEAD = {0: 1, 1: 3, 3: 5}
BEHIND = {0: 2, 2: 4, 4: 6}
TAIL = 7 * CHUNK
OWN = (0, 1024, 1536, 3072, 3584, 5120, 5632, TAIL + 128)
SIB = (512, 2048, 2560, 4096, 4608, 6144, 6656, TAIL + 640)
WINDOW = ((TAIL, 128), (TAIL + 1152, 128), (TAIL + 1280, 256), (TAIL + 1536, 256))
STEPS = ((0, 1), (1, 3), (3, 5), (5, 7))
PARTS = ((0, 0), (0, 1), (1, 0), (1, 1))
KEY_PARTS, VALUE_PARTS = PARTS[:2], PARTS[2:]


def moves_of(parts, *chunks):
    return tuple((kind, part, r) for kind, part in parts for r in chunks)


FIRST = moves_of(PARTS, 0) + moves_of(KEY_PARTS, 1, 2)
RELAYS = {
    (0, 3): moves_of(VALUE_PARTS, 1, 2),
    (1, 5): moves_of(PARTS, 3, 4) + ("send",),
    (2, 5): moves_of(PARTS, 5, 6),
    (3, 4): ("cross",) + moves_of(PARTS, 7),
}
ANSWERS = ((0, 0, 7), (1, 0, 4), (1, 4, 7))
MESH = pl.DeviceIdType.MESH


def kernel(
    pk, pv, rq, rk, rv, seg, plen, out,
    qbuf, kbuf, vbuf, segsrc, segbuf, acc, peak, obuf, bias0,
    q_send, q_recv, rkv_recv, st_send, st_recv,
    ring_send, ring_recv, sib_send, sib_recv,
    fw_send, fw_recv, o_send, o_recv,
):
    gi = lax.axis_index("grp")
    si = lax.axis_index("seq")
    x, c = lax.div(gi, 2), lax.rem(gi, 2)
    z, y = lax.div(si, YS), lax.rem(si, YS)
    yh, yl = lax.div(y, 2), lax.rem(y, 2)
    zn, zp = lax.rem(z + 1, ZS), lax.rem(z + ZS - 1, ZS)
    mine = yh == c
    ahead = (gi, zn * YS + y)
    behind = (gi, zp * YS + y)
    sibling = (2 * x + 1 - c, si)

    barrier = pltpu.get_barrier_semaphore()

    def greet(i, carry):
        s, g = lax.div(i, 8), lax.rem(i, 8)
        who = z * YS + 2 * c + s

        @pl.when(jnp.logical_or(g != gi, who != si))
        def _():
            pl.semaphore_signal(barrier, inc=1, device_id=(g, who), device_id_type=MESH)

        return carry

    lax.fori_loop(0, 16, greet, 0)
    for who in (ahead, behind, sibling):
        pl.semaphore_signal(barrier, inc=1, device_id=who, device_id_type=MESH)
    segsrc[...] = jnp.full((8, 128), plen[0], jnp.int32)
    segsrc[0:1, :] = seg[...]
    pl.semaphore_wait(barrier, jnp.where(mine, 18, 19))

    def remote(src, dst, send, recv, who):
        return pltpu.make_async_remote_copy(
            src_ref=src, dst_ref=dst, send_sem=send, recv_sem=recv,
            device_id=who, device_id_type=MESH,
        )

    def put(src, dst, send, recv, who, here):
        @pl.when(here)
        def _():
            pltpu.make_async_copy(src, dst, recv).start()

        @pl.when(jnp.logical_not(here))
        def _():
            remote(src, dst, send, recv, who).start()

    def sent(src, dst, send, recv, who, here):
        @pl.when(jnp.logical_not(here))
        def _():
            remote(src, dst, send, recv, who).wait_send()

    def arrived(ref, sem):
        pltpu.make_async_copy(ref, ref, sem).wait()

    def keys_at(start, count):
        return kbuf.at[pl.ds(start, count), :]

    def values_at(start, count):
        return vbuf.at[pl.ds(start, count), pl.ds(0, HD)]

    own_at = pl.multiple_of(OWN[0] + yl * SHARD, SHARD)

    def staged(h):
        who = (2 * x + yh, z * YS + 2 * c + h)
        here = jnp.logical_and(mine, yl == h)
        cols = pl.ds(h * HD, HD)
        return (
            (pk.at[0, :, cols], keys_at(own_at, SHARD), st_send.at[0, h], st_recv.at[0, yl], who, here),
            (pv.at[0, :, cols], values_at(own_at, SHARD), st_send.at[1, h], st_recv.at[1, yl], who, here),
            (segsrc, segbuf.at[2, yl], st_send.at[2, h], st_recv.at[2, yl], who, here),
        )

    row_at = pl.multiple_of(yl * 128 + gi * 16, 16)

    def queried(i):
        tx = lax.rem(x + 1 + lax.div(i, 4), XS)
        ty = lax.rem(y + 1 + lax.rem(i, 4), YS)
        th = lax.div(ty, 2)
        tl = lax.rem(ty, 2)
        g = 2 * tx + th
        who = (2 * tx + yh, z * YS + ty)
        here = jnp.logical_and(mine, i == 15)
        wide = pl.ds(pl.multiple_of(tl * WIDE, 128), WIDE)
        cols = pl.ds(pl.multiple_of(tl * HD, 128), HD)
        at = pl.multiple_of(WINDOW[3][0] + row_at, 16)
        return (
            (rq.at[g, :, wide], qbuf.at[pl.ds(row_at, 16), :], q_send.at[0, i], q_recv, who, here),
            (rk.at[g, :, cols], keys_at(at, 16), q_send.at[1, i], rkv_recv.at[0], who, here),
            (rv.at[g, :, cols], values_at(at, 16), q_send.at[2, i], rkv_recv.at[1], who, here),
        )

    def send_queries(i, carry):
        put(*queried(i)[0])
        return carry

    def send_rest(i, carry):
        put(*queried(i)[1])
        put(*queried(i)[2])
        return carry

    for part in range(3):
        for h in range(2):
            put(*staged(h)[part])
    lax.fori_loop(0, 16, send_queries, 0)
    lax.fori_loop(0, 16, send_rest, 0)

    def ones(i, carry):
        vbuf[pl.ds(pl.multiple_of(i * 256, 256), 256), HD:] = jnp.ones((256, HD), jnp.bfloat16)
        return carry

    lax.fori_loop(0, KEYS // 256, ones, 0)

    def rows_of(kind, start, count):
        return keys_at(start, count) if kind == 0 else values_at(start, count)

    def piece_at(kind, start, part):
        return rows_of(kind, start + part * SHARD, SHARD)

    def onward(kind, part, r):
        here = piece_at(kind, OWN[r], part)
        moves = [(way[r], who) for way, who in ((AHEAD, ahead), (BEHIND, behind)) if r in way]
        if (r == 5 and (kind, part) == (0, 0)) or (r == 6 and (kind, part) != (0, 0)):
            moves.append((7, ahead if r == 5 else behind))
        copies = [
            remote(here, piece_at(kind, OWN[to], part), ring_send.at[kind, part, to],
                   ring_recv.at[kind, part, to], who)
            for to, who in moves
        ]
        copies.append(remote(
            here, piece_at(kind, SIB[r], part), sib_send.at[kind, part, r],
            sib_recv.at[kind, part, r], sibling,
        ))
        return copies

    def relay(kind, part, r):
        sem = st_recv.at[kind, part] if r == 0 else ring_recv.at[kind, part, r]
        arrived(piece_at(kind, OWN[r], part), sem)
        for copy in onward(kind, part, r):
            copy.start()

    def from_sibling(r):
        for kind in range(2):
            for part in range(2):
                arrived(piece_at(kind, SIB[r], part), sib_recv.at[kind, part, r])

    for item in FIRST:
        relay(*item)

    def forwards():
        copies = []
        for kind in range(2):
            for part in range(2):
                src = WINDOW[3][0] + 128 * part
                copies.append(remote(
                    rows_of(kind, src, 128), rows_of(kind, WINDOW[part][0], 128),
                    fw_send.at[kind, part], fw_recv.at[kind, part], ahead,
                ))
        copies.append(
            remote(segbuf.at[2], segbuf.at[0], fw_send.at[2, 0], fw_recv.at[2, 0], ahead)
        )
        return copies

    def crossings():
        copies = []
        for kind in range(2):
            for part in range(2):
                src = jnp.where(c == 0, WINDOW[3][0] + 128 * part, WINDOW[part][0])
                src = pl.multiple_of(src, 128)
                copies.append(remote(
                    rows_of(kind, src, 128), rows_of(kind, WINDOW[2][0] + 128 * part, 128),
                    fw_send.at[kind, 2 + part], fw_recv.at[kind, 2 + part], sibling,
                ))
        src = segbuf.at[jnp.where(c == 0, 2, 0)]
        copies.append(remote(src, segbuf.at[1], fw_send.at[2, 1], fw_recv.at[2, 1], sibling))
        return copies

    def send_window():
        for kind in range(2):
            arrived(rows_of(kind, *WINDOW[3]), rkv_recv.at[kind])
        for copy in forwards():
            copy.start()

    def cross_window():
        for kind in range(2):
            for part in range(2):
                arrived(rows_of(kind, *WINDOW[part]), fw_recv.at[kind, part])
        arrived(segbuf.at[0], fw_recv.at[2, 0])
        for copy in crossings():
            copy.start()

    def take_window():
        for kind in range(2):
            for part in range(2):
                start = WINDOW[2][0] + 128 * part
                arrived(rows_of(kind, start, 128), fw_recv.at[kind, 2 + part])
        arrived(segbuf.at[1], fw_recv.at[2, 1])
        first = 512 * z + 256 * c - 512
        row = lax.broadcasted_iota(jnp.int32, (128, 128), 0)
        col = lax.broadcasted_iota(jnp.int32, (128, 128), 1)
        for a in range(2):
            ids = jnp.broadcast_to(segbuf[2, a, 0:1, :].astype(jnp.float32), (128, 128))
            ids = jnp.transpose(ids)
            for j in range(WIN // 128):
                theirs = segbuf[j // 2, j % 2, 0:1, :].astype(jnp.float32)
                before = (j * 128 + col <= 512 + a * 128 + row) & (first + j * 128 + col >= 0)
                bias0[a * 128:(a + 1) * 128, j * 128:(j + 1) * 128] = jnp.where(
                    before & (ids == theirs), 0.0, MASKED
                ).astype(jnp.float32)

    lane = lax.broadcasted_iota(jnp.int32, (1, 128), 1)

    def prompt_bias(r, half):
        limit = segbuf[2, 0, 1:2, :]
        base = lax.rem(z + ZS + DELTA[r], ZS) * CHUNK + half * HALF
        return [
            jnp.where(base + j * 128 + lane < limit, 0.0, MASKED).astype(jnp.float32)
            for j in range(HALF // 128)
        ]

    def weigh(lo, count, rows, h, bias):
        q = qbuf[rows, h * HD:(h + 1) * HD]
        s = lax.dot_general(
            q, kbuf[lo:lo + count, :], (((1,), (1,)), ((), ())),
            preferred_element_type=jnp.float32,
        )
        return s + bias

    def numerators(s, top):
        return jnp.exp2((s - top[:, :1]) * LOG2).astype(jnp.bfloat16)

    def product(p, lo, count):
        return jnp.dot(p, vbuf[lo:lo + count, :], preferred_element_type=jnp.float32)

    def carry_on(item):
        if item == "send":
            send_window()
        elif item == "cross":
            cross_window()
        else:
            relay(*item)

    for j in range(2):
        arrived(segbuf.at[2, j], st_recv.at[2, j])
    arrived(qbuf, q_recv)

    for step, (a, b) in enumerate(STEPS):
        for r in range(a, b):
            from_sibling(r)
        pieces = [
            piece
            for half in (c, 1 - c)
            for r in range(a, b)
            for piece in prompt_bias(r, half)
        ]
        bias = jnp.concatenate(pieces, axis=1)
        lo, count = a * CHUNK, (b - a) * CHUNK
        for h in range(HG):
            rows = slice(0, ROWS)
            s = weigh(lo, count, rows, h, bias)
            top = jnp.max(s, axis=1, keepdims=True)
            if step == 0:
                top = jnp.broadcast_to(top, (ROWS, HD))
                acc[h] = product(numerators(s, top), lo, count)
            else:
                old = peak[h]
                top = jnp.maximum(old, top)
                fade = jnp.exp2((old - top) * LOG2)
                got = product(numerators(s, top), lo, count)
                acc[h, :, :HD] = acc[h, :, :HD] * fade + got[:, :HD]
                acc[h, :, HD:] = acc[h, :, HD:] * fade + got[:, HD:]
            peak[h] = top
            for item in RELAYS.get((step, h), ()):
                carry_on(item)

    def answer(n):
        a_half, h0, h1 = ANSWERS[n]
        who = (2 * x + yh, z * YS + 2 * c + a_half)
        here = jnp.logical_and(mine, yl == a_half)
        width = (h1 - h0) * HD
        cols = pl.ds(pl.multiple_of(yl * WIDE + h0 * HD, 128), width)
        src = obuf.at[a_half, :, pl.ds(h0 * HD, width)]
        return (src, out.at[0, :, cols], o_send.at[n], o_recv, who, here)

    take_window()
    from_sibling(7)
    pieces = [piece for half in (c, 1 - c) for piece in prompt_bias(7, half)]
    late = jnp.broadcast_to(jnp.concatenate(pieces, axis=1), (128, CHUNK))
    for a_half in range(2):
        rows = slice(a_half * 128, a_half * 128 + 128)
        if a_half == 0:
            lo = TAIL
            bias = jnp.concatenate([bias0[rows, 0:128], late, bias0[rows, 128:640]], axis=1)
        else:
            lo = TAIL + 128
            bias = jnp.concatenate([late, bias0[rows, 128:]], axis=1)
        count = CHUNK + 640
        for h in range(HG):
            s = weigh(lo, count, rows, h, bias)
            old = peak[h, rows, :]
            top = jnp.maximum(old, jnp.max(s, axis=1, keepdims=True))
            fade = jnp.exp2((old - top) * LOG2)
            got = product(numerators(s, top), lo, count)
            weighted = acc[h, rows, :HD] * fade + got[:, :HD]
            total = acc[h, rows, HD:] * fade + got[:, HD:]
            obuf[a_half, :, h * HD:(h + 1) * HD] = (weighted / total).astype(jnp.bfloat16)
            for n, (half, _, stop) in enumerate(ANSWERS):
                if (half, stop) == (a_half, h + 1):
                    put(*answer(n))

    for n in range(len(ANSWERS)):
        sent(*answer(n))
    for h in range(2):
        for item in staged(h):
            sent(*item)

    def settle(i, carry):
        for item in queried(i):
            sent(*item)
        return carry

    lax.fori_loop(0, 16, settle, 0)
    for r in range(ZS):
        for kind in range(2):
            for part in range(2):
                for copy in onward(kind, part, r):
                    copy.wait_send()
    for copy in forwards() + crossings():
        copy.wait_send()
    arrived(out, o_recv)


def body(
    prompt_keys, prompt_values, resp_queries, resp_keys, resp_values, segment_ids, prompt_lengths
):
    dma = pltpu.SemaphoreType.DMA
    held = pl.BlockSpec(memory_space=pl.ANY)
    return pl.pallas_call(
        kernel,
        out_shape=jax.ShapeDtypeStruct((1, 128, H * HD), jnp.bfloat16),
        in_specs=[held] * 5
        + [pl.BlockSpec(memory_space=pltpu.VMEM), pl.BlockSpec(memory_space=pltpu.SMEM)],
        out_specs=held,
        scratch_shapes=[
            pltpu.VMEM((ROWS, WIDE), jnp.bfloat16),
            pltpu.VMEM((KEYS, HD), jnp.bfloat16),
            pltpu.VMEM((KEYS, 2 * HD), jnp.bfloat16),
            pltpu.VMEM((8, 128), jnp.int32),
            pltpu.VMEM((3, 2, 8, 128), jnp.int32),
            pltpu.VMEM((HG, ROWS, 2 * HD), jnp.float32),
            pltpu.VMEM((HG, ROWS, HD), jnp.float32),
            pltpu.VMEM((2, 128, WIDE), jnp.bfloat16),
            pltpu.VMEM((ROWS, WIN), jnp.float32),
            dma((3, 16)),
            dma,
            dma((2,)),
            dma((3, 2)),
            dma((3, 2)),
            dma((2, 2, ZS)),
            dma((2, 2, ZS)),
            dma((2, 2, ZS)),
            dma((2, 2, ZS)),
            dma((3, 4)),
            dma((3, 4)),
            dma((len(ANSWERS),)),
            dma,
        ],
        compiler_params=pltpu.CompilerParams(
            collective_id=0, has_side_effects=True, vmem_limit_bytes=60 << 20
        ),
        name="shared_prompt_attention",
    )(prompt_keys, prompt_values, resp_queries, resp_keys, resp_values, segment_ids, prompt_lengths)


def solution(mesh):
    in_specs = (
        P("grp", "seq", None),
        P("grp", "seq", None),
        P(None, ("seq", "grp"), None),
        P(None, ("seq", "grp"), None),
        P(None, ("seq", "grp"), None),
        P("grp", "seq"),
        P("grp"),
    )
    out_specs = P("grp", "seq", None)
    return jax.shard_map(body, mesh=mesh, in_specs=in_specs, out_specs=out_specs, check_vma=False)
```

```python
import math

import jax
import jax.numpy as jnp
from jax import lax
from jax.experimental import pallas as pl
from jax.experimental.pallas import tpu as pltpu
from jax.sharding import PartitionSpec as P

HD = 128
H = 14
KVH = 2
HG = H // KVH
WIDE = HG * HD
XS, YS, ZS = 4, 4, 8
ROWS = 256
WIN = 3 * ROWS
SHARD = 256
HALF = 2 * SHARD
CHUNK = 2 * HALF
KEYS = WIN + ZS * CHUNK
MASKED = -1e30
LOG2 = math.log2(math.e) / math.sqrt(HD)
DELTA = (0, -1, 1, -2, 2, -3, 3, 4)
AHEAD = {0: 1, 1: 3, 3: 5}
BEHIND = {0: 2, 2: 4, 4: 6}
TAIL = 7 * CHUNK
OWN = (0, 1024, 1536, 3072, 3584, 5120, 5632, TAIL + 128)
SIB = (512, 2048, 2560, 4096, 4608, 6144, 6656, TAIL + 640)
WINDOW = ((TAIL, 128), (TAIL + 1152, 128), (TAIL + 1280, 256), (TAIL + 1536, 256))
STEPS = ((0, 1), (1, 3), (3, 5), (5, 7))
PARTS = ((0, 0), (0, 1), (1, 0), (1, 1))
KEY_PARTS, VALUE_PARTS = PARTS[:2], PARTS[2:]


def moves_of(parts, *chunks):
    return tuple((kind, part, r) for kind, part in parts for r in chunks)


FIRST = moves_of(PARTS, 0) + moves_of(KEY_PARTS, 1, 2)
RELAYS = {
    (0, 3): moves_of(VALUE_PARTS, 1, 2),
    (1, 5): moves_of(PARTS, 3, 4) + ("send",),
    (2, 5): moves_of(PARTS, 5, 6) + ("cross",),
    (3, 4): moves_of(PARTS, 7) + ("take",),
}
ANSWERS = ((0, 0, 7), (1, 0, 4), (1, 4, 7))
MESH = pl.DeviceIdType.MESH


def kernel(
    pk, pv, rq, rk, rv, seg, plen, out,
    qbuf, kbuf, vbuf, segsrc, segbuf, acc, peak, obuf, bias0,
    q_send, q_recv, rkv_recv, st_send, st_recv,
    ring_send, ring_recv, sib_send, sib_recv,
    fw_send, fw_recv, o_send, o_recv,
):
    gi = lax.axis_index("grp")
    si = lax.axis_index("seq")
    x, c = lax.div(gi, 2), lax.rem(gi, 2)
    z, y = lax.div(si, YS), lax.rem(si, YS)
    yh, yl = lax.div(y, 2), lax.rem(y, 2)
    zn, zp = lax.rem(z + 1, ZS), lax.rem(z + ZS - 1, ZS)
    mine = yh == c
    ahead = (gi, zn * YS + y)
    behind = (gi, zp * YS + y)
    sibling = (2 * x + 1 - c, si)

    barrier = pltpu.get_barrier_semaphore()

    def greet(i, carry):
        s, g = lax.div(i, 8), lax.rem(i, 8)
        who = z * YS + 2 * c + s

        @pl.when(jnp.logical_or(g != gi, who != si))
        def _():
            pl.semaphore_signal(barrier, inc=1, device_id=(g, who), device_id_type=MESH)

        return carry

    lax.fori_loop(0, 16, greet, 0)
    for who in (ahead, behind, sibling):
        pl.semaphore_signal(barrier, inc=1, device_id=who, device_id_type=MESH)
    segsrc[...] = jnp.full((8, 128), plen[0], jnp.int32)
    segsrc[0:1, :] = seg[...]
    pl.semaphore_wait(barrier, jnp.where(mine, 18, 19))

    def remote(src, dst, send, recv, who):
        return pltpu.make_async_remote_copy(
            src_ref=src, dst_ref=dst, send_sem=send, recv_sem=recv,
            device_id=who, device_id_type=MESH,
        )

    def put(src, dst, send, recv, who, here):
        @pl.when(here)
        def _():
            pltpu.make_async_copy(src, dst, recv).start()

        @pl.when(jnp.logical_not(here))
        def _():
            remote(src, dst, send, recv, who).start()

    def sent(src, dst, send, recv, who, here):
        @pl.when(jnp.logical_not(here))
        def _():
            remote(src, dst, send, recv, who).wait_send()

    def arrived(ref, sem):
        pltpu.make_async_copy(ref, ref, sem).wait()

    def keys_at(start, count):
        return kbuf.at[pl.ds(start, count), :]

    def values_at(start, count):
        return vbuf.at[pl.ds(start, count), pl.ds(0, HD)]

    own_at = pl.multiple_of(OWN[0] + yl * SHARD, SHARD)

    def staged(h):
        who = (2 * x + yh, z * YS + 2 * c + h)
        here = jnp.logical_and(mine, yl == h)
        cols = pl.ds(h * HD, HD)
        return (
            (pk.at[0, :, cols], keys_at(own_at, SHARD), st_send.at[0, h], st_recv.at[0, yl], who, here),
            (pv.at[0, :, cols], values_at(own_at, SHARD), st_send.at[1, h], st_recv.at[1, yl], who, here),
            (segsrc, segbuf.at[2, yl], st_send.at[2, h], st_recv.at[2, yl], who, here),
        )

    row_at = pl.multiple_of(yl * 128 + gi * 16, 16)

    def queried(i):
        tx = lax.rem(x + 1 + lax.div(i, 4), XS)
        ty = lax.rem(y + 1 + lax.rem(i, 4), YS)
        th = lax.div(ty, 2)
        tl = lax.rem(ty, 2)
        g = 2 * tx + th
        who = (2 * tx + yh, z * YS + ty)
        here = jnp.logical_and(mine, i == 15)
        wide = pl.ds(pl.multiple_of(tl * WIDE, 128), WIDE)
        cols = pl.ds(pl.multiple_of(tl * HD, 128), HD)
        at = pl.multiple_of(WINDOW[3][0] + row_at, 16)
        return (
            (rq.at[g, :, wide], qbuf.at[pl.ds(row_at, 16), :], q_send.at[0, i], q_recv, who, here),
            (rk.at[g, :, cols], keys_at(at, 16), q_send.at[1, i], rkv_recv.at[0], who, here),
            (rv.at[g, :, cols], values_at(at, 16), q_send.at[2, i], rkv_recv.at[1], who, here),
        )

    def send_queries(i, carry):
        put(*queried(i)[0])
        return carry

    def send_rest(i, carry):
        put(*queried(i)[1])
        put(*queried(i)[2])
        return carry

    for part in range(3):
        for h in range(2):
            put(*staged(h)[part])
    lax.fori_loop(0, 16, send_queries, 0)
    lax.fori_loop(0, 16, send_rest, 0)

    def ones(i, carry):
        vbuf[pl.ds(pl.multiple_of(i * 256, 256), 256), HD:] = jnp.ones((256, HD), jnp.bfloat16)
        return carry

    lax.fori_loop(0, KEYS // 256, ones, 0)

    def rows_of(kind, start, count):
        return keys_at(start, count) if kind == 0 else values_at(start, count)

    def piece_at(kind, start, part):
        return rows_of(kind, start + part * SHARD, SHARD)

    def onward(kind, part, r):
        here = piece_at(kind, OWN[r], part)
        moves = [(way[r], who) for way, who in ((AHEAD, ahead), (BEHIND, behind)) if r in way]
        if (r == 5 and (kind, part) == (0, 0)) or (r == 6 and (kind, part) != (0, 0)):
            moves.append((7, ahead if r == 5 else behind))
        copies = [
            remote(here, piece_at(kind, OWN[to], part), ring_send.at[kind, part, to],
                   ring_recv.at[kind, part, to], who)
            for to, who in moves
        ]
        copies.append(remote(
            here, piece_at(kind, SIB[r], part), sib_send.at[kind, part, r],
            sib_recv.at[kind, part, r], sibling,
        ))
        return copies

    def relay(kind, part, r):
        sem = st_recv.at[kind, part] if r == 0 else ring_recv.at[kind, part, r]
        arrived(piece_at(kind, OWN[r], part), sem)
        for copy in onward(kind, part, r):
            copy.start()

    def from_sibling(r):
        for kind in range(2):
            for part in range(2):
                arrived(piece_at(kind, SIB[r], part), sib_recv.at[kind, part, r])

    for item in FIRST:
        relay(*item)

    def forwards():
        copies = []
        for kind in range(2):
            for part in range(2):
                src = WINDOW[3][0] + 128 * part
                copies.append(remote(
                    rows_of(kind, src, 128), rows_of(kind, WINDOW[part][0], 128),
                    fw_send.at[kind, part], fw_recv.at[kind, part], ahead,
                ))
        copies.append(
            remote(segbuf.at[2], segbuf.at[0], fw_send.at[2, 0], fw_recv.at[2, 0], ahead)
        )
        return copies

    def crossings():
        copies = []
        for kind in range(2):
            for part in range(2):
                src = jnp.where(c == 0, WINDOW[3][0] + 128 * part, WINDOW[part][0])
                src = pl.multiple_of(src, 128)
                copies.append(remote(
                    rows_of(kind, src, 128), rows_of(kind, WINDOW[2][0] + 128 * part, 128),
                    fw_send.at[kind, 2 + part], fw_recv.at[kind, 2 + part], sibling,
                ))
        src = segbuf.at[jnp.where(c == 0, 2, 0)]
        copies.append(remote(src, segbuf.at[1], fw_send.at[2, 1], fw_recv.at[2, 1], sibling))
        return copies

    def send_window():
        for kind in range(2):
            arrived(rows_of(kind, *WINDOW[3]), rkv_recv.at[kind])
        for copy in forwards():
            copy.start()

    def cross_window():
        for kind in range(2):
            for part in range(2):
                arrived(rows_of(kind, *WINDOW[part]), fw_recv.at[kind, part])
        arrived(segbuf.at[0], fw_recv.at[2, 0])
        for copy in crossings():
            copy.start()

    def take_window():
        for kind in range(2):
            for part in range(2):
                start = WINDOW[2][0] + 128 * part
                arrived(rows_of(kind, start, 128), fw_recv.at[kind, 2 + part])
        arrived(segbuf.at[1], fw_recv.at[2, 1])
        first = 512 * z + 256 * c - 512
        row = lax.broadcasted_iota(jnp.int32, (128, 128), 0)
        col = lax.broadcasted_iota(jnp.int32, (128, 128), 1)
        for a in range(2):
            ids = jnp.broadcast_to(segbuf[2, a, 0:1, :].astype(jnp.float32), (128, 128))
            ids = jnp.transpose(ids)
            for j in range(WIN // 128):
                theirs = segbuf[j // 2, j % 2, 0:1, :].astype(jnp.float32)
                before = (j * 128 + col <= 512 + a * 128 + row) & (first + j * 128 + col >= 0)
                bias0[a * 128:(a + 1) * 128, j * 128:(j + 1) * 128] = jnp.where(
                    before & (ids == theirs), 0.0, MASKED
                ).astype(jnp.float32)

    lane = lax.broadcasted_iota(jnp.int32, (1, 128), 1)

    def prompt_bias(r, half):
        limit = segbuf[2, 0, 1:2, :]
        base = lax.rem(z + ZS + DELTA[r], ZS) * CHUNK + half * HALF
        return [
            jnp.where(base + j * 128 + lane < limit, 0.0, MASKED).astype(jnp.float32)
            for j in range(HALF // 128)
        ]

    def weigh(lo, count, rows, h, bias):
        q = qbuf[rows, h * HD:(h + 1) * HD]
        s = lax.dot_general(
            q, kbuf[lo:lo + count, :], (((1,), (1,)), ((), ())),
            preferred_element_type=jnp.float32,
        )
        return s + bias

    def numerators(s, top):
        return jnp.exp2((s - top[:, :1]) * LOG2).astype(jnp.bfloat16)

    def product(p, lo, count):
        return jnp.dot(p, vbuf[lo:lo + count, :], preferred_element_type=jnp.float32)

    def carry_on(item):
        if item == "send":
            send_window()
        elif item == "cross":
            cross_window()
        elif item == "take":
            take_window()
        else:
            relay(*item)

    for j in range(2):
        arrived(segbuf.at[2, j], st_recv.at[2, j])
    arrived(qbuf, q_recv)

    for step, (a, b) in enumerate(STEPS):
        for r in range(a, b):
            from_sibling(r)
        pieces = [
            piece
            for half in (c, 1 - c)
            for r in range(a, b)
            for piece in prompt_bias(r, half)
        ]
        bias = jnp.concatenate(pieces, axis=1)
        lo, count = a * CHUNK, (b - a) * CHUNK
        for h in range(HG):
            rows = slice(0, ROWS)
            s = weigh(lo, count, rows, h, bias)
            top = jnp.max(s, axis=1, keepdims=True)
            if step == 0:
                top = jnp.broadcast_to(top, (ROWS, HD))
                acc[h] = product(numerators(s, top), lo, count)
            else:
                old = peak[h]
                top = jnp.maximum(old, top)
                fade = jnp.exp2((old - top) * LOG2)
                got = product(numerators(s, top), lo, count)
                acc[h, :, :HD] = acc[h, :, :HD] * fade + got[:, :HD]
                acc[h, :, HD:] = acc[h, :, HD:] * fade + got[:, HD:]
            peak[h] = top
            for item in RELAYS.get((step, h), ()):
                carry_on(item)

    def answer(n):
        a_half, h0, h1 = ANSWERS[n]
        who = (2 * x + yh, z * YS + 2 * c + a_half)
        here = jnp.logical_and(mine, yl == a_half)
        width = (h1 - h0) * HD
        cols = pl.ds(pl.multiple_of(yl * WIDE + h0 * HD, 128), width)
        src = obuf.at[a_half, :, pl.ds(h0 * HD, width)]
        return (src, out.at[0, :, cols], o_send.at[n], o_recv, who, here)

    from_sibling(7)
    pieces = [piece for half in (c, 1 - c) for piece in prompt_bias(7, half)]
    late = jnp.broadcast_to(jnp.concatenate(pieces, axis=1), (128, CHUNK))
    for a_half in range(2):
        rows = slice(a_half * 128, a_half * 128 + 128)
        if a_half == 0:
            lo = TAIL
            bias = jnp.concatenate([bias0[rows, 0:128], late, bias0[rows, 128:640]], axis=1)
        else:
            lo = TAIL + 128
            bias = jnp.concatenate([late, bias0[rows, 128:]], axis=1)
        count = CHUNK + 640
        for h in range(HG):
            s = weigh(lo, count, rows, h, bias)
            old = peak[h, rows, :]
            top = jnp.maximum(old, jnp.max(s, axis=1, keepdims=True))
            fade = jnp.exp2((old - top) * LOG2)
            got = product(numerators(s, top), lo, count)
            weighted = acc[h, rows, :HD] * fade + got[:, :HD]
            total = acc[h, rows, HD:] * fade + got[:, HD:]
            obuf[a_half, :, h * HD:(h + 1) * HD] = (weighted / total).astype(jnp.bfloat16)
            for n, (half, _, stop) in enumerate(ANSWERS):
                if (half, stop) == (a_half, h + 1):
                    put(*answer(n))

    for n in range(len(ANSWERS)):
        sent(*answer(n))
    for h in range(2):
        for item in staged(h):
            sent(*item)

    def settle(i, carry):
        for item in queried(i):
            sent(*item)
        return carry

    lax.fori_loop(0, 16, settle, 0)
    for r in range(ZS):
        for kind in range(2):
            for part in range(2):
                for copy in onward(kind, part, r):
                    copy.wait_send()
    for copy in forwards() + crossings():
        copy.wait_send()
    arrived(out, o_recv)


def body(
    prompt_keys, prompt_values, resp_queries, resp_keys, resp_values, segment_ids, prompt_lengths
):
    dma = pltpu.SemaphoreType.DMA
    held = pl.BlockSpec(memory_space=pl.ANY)
    return pl.pallas_call(
        kernel,
        out_shape=jax.ShapeDtypeStruct((1, 128, H * HD), jnp.bfloat16),
        in_specs=[held] * 5
        + [pl.BlockSpec(memory_space=pltpu.VMEM), pl.BlockSpec(memory_space=pltpu.SMEM)],
        out_specs=held,
        scratch_shapes=[
            pltpu.VMEM((ROWS, WIDE), jnp.bfloat16),
            pltpu.VMEM((KEYS, HD), jnp.bfloat16),
            pltpu.VMEM((KEYS, 2 * HD), jnp.bfloat16),
            pltpu.VMEM((8, 128), jnp.int32),
            pltpu.VMEM((3, 2, 8, 128), jnp.int32),
            pltpu.VMEM((HG, ROWS, 2 * HD), jnp.float32),
            pltpu.VMEM((HG, ROWS, HD), jnp.float32),
            pltpu.VMEM((2, 128, WIDE), jnp.bfloat16),
            pltpu.VMEM((ROWS, WIN), jnp.float32),
            dma((3, 16)),
            dma,
            dma((2,)),
            dma((3, 2)),
            dma((3, 2)),
            dma((2, 2, ZS)),
            dma((2, 2, ZS)),
            dma((2, 2, ZS)),
            dma((2, 2, ZS)),
            dma((3, 4)),
            dma((3, 4)),
            dma((len(ANSWERS),)),
            dma,
        ],
        compiler_params=pltpu.CompilerParams(
            collective_id=0, has_side_effects=True, vmem_limit_bytes=60 << 20
        ),
        name="shared_prompt_attention",
    )(prompt_keys, prompt_values, resp_queries, resp_keys, resp_values, segment_ids, prompt_lengths)


def solution(mesh):
    in_specs = (
        P("grp", "seq", None),
        P("grp", "seq", None),
        P(None, ("seq", "grp"), None),
        P(None, ("seq", "grp"), None),
        P(None, ("seq", "grp"), None),
        P("grp", "seq"),
        P("grp"),
    )
    out_specs = P("grp", "seq", None)
    return jax.shard_map(body, mesh=mesh, in_specs=in_specs, out_specs=out_specs, check_vma=False)
```
